32 devices in a mesh: dom: 8 (over y, x, core), rep: 4 (over z).
Axes of the slice: x: 2, y: 2, z: 4, core: 2. Of those that a mesh axis runs over, the one named last changes fastest.
Arguments:
- features: float32 [2048, 256], P('dom'), may hold values from -6 to 6
- tile_values: bfloat16 [8, 64, 128, 128], P('dom', 'rep'), may hold values from 0 to 0.03125
- tile_rows: int32 [8, 64], P('dom', 'rep'), may hold values from 0 to 1
- tile_cols: int32 [8, 64], P('dom', 'rep'), may hold values from 0 to 15, as said below
- weight: float32 [256, 256], replicated, may hold values from -0.375 to 0.375
- bias: float32 [256], replicated, may hold values from -3 to 3
- cotangent: float32 [2048, 256], P('dom'), may hold values from -6 to 6
Outputs:
- activations: float32 [2048, 256], P('dom')
- grad_features: float32 [2048, 256], P('dom')
- grad_weight: float32 [256, 256], replicated
- grad_bias: float32 [256], replicated
The draws below stay inside these ranges and needn't reach their ends.
Inputs may be any that keep to these rules, and one draw needn't show every extreme that they name: `tile_cols`: within each share of 16 consecutive tiles of a partition, every tile column 0 to 15 appears exactly once.
All inputs are finite; a program needn't handle non-finite values.
Results may differ from the reference program's by a relative error of at most 0.0003.
Values sent between devices are 32-bit elements; how exact they have to be, the bound alone decides.
A program may use at most 64 MiB of HBM per device.

```python
import jax
import jax.numpy as jnp
from jax import lax

F = 256
TILE = 128
ROW_BLOCKS = 2
PARTS_SIZE = 8
ROWS = 256
NODES = 2048
COL_BLOCKS = 16
SLOTS = 16
SHARE = 64
N_REP = 4


def draw_tile_cols(key, part):
    groups = PARTS_SIZE * (SHARE // SLOTS)
    keys = jax.random.split(jax.random.fold_in(key, 17), groups)
    orders = jax.vmap(lambda single: jax.random.permutation(single, COL_BLOCKS))(keys)
    return orders.astype(jnp.int32).reshape(PARTS_SIZE, SHARE)


def set_ends(result, stream_key, low, top_value):
    dims = result.shape
    spot = [jax.random.randint(jax.random.fold_in(stream_key, axis), (), 0, dims[axis]) for axis in range(len(dims))]
    result = result.at[tuple(spot)].set(low)
    longest = dims.index(max(dims))
    spot[longest] = (spot[longest] + 1) % dims[longest]
    return result.at[tuple(spot)].set(top_value)


def block_scale(rng, extent, cuts, low, high):
    loudness, own = 1.0, jax.random.fold_in(rng, 6)
    for axis_at, parts in cuts:
        heights = jnp.exp(jax.random.uniform(jax.random.fold_in(own, axis_at), (parts,), jnp.float32, low / len(cuts), high / len(cuts)))
        loudness = loudness * jnp.repeat(heights, extent[axis_at] // parts).reshape([-1 if axis == axis_at else 1 for axis in range(len(extent))])
    return loudness


def normal_values(stream_key, extent, spread, most, shards=(), held_as=jnp.bfloat16):
    values = spread * jax.random.normal(stream_key, extent, jnp.float32)
    if shards:
        values = values * block_scale(stream_key, extent, shards, -0.22, 0.18)
    return jnp.clip(values, -most, most).astype(held_as)


def setup_inputs(seed: int = 0) -> dict:
    splits = jax.random.split(jax.random.key(seed), 8)
    features = normal_values(splits[0], (NODES, F), 1.0, 6.0, ((0, 8),), jnp.float32)
    tile_values = jnp.clip(0.03125 * jax.random.uniform(splits[1], (PARTS_SIZE, SHARE, TILE, TILE), jnp.float32) ** block_scale(splits[1], (PARTS_SIZE, SHARE, TILE, TILE), ((0, 8), (1, 4)), -0.2, 0.2), 0.0, 0.03125).astype(jnp.bfloat16)
    tile_rows = set_ends(jax.random.randint(splits[2], (PARTS_SIZE, SHARE), 0, ROW_BLOCKS), jax.random.fold_in(splits[2], 1), 0, ROW_BLOCKS - 1).astype(jnp.int32)
    tile_cols = draw_tile_cols(jax.random.fold_in(splits[7], 71), 0)
    weight = normal_values(splits[4], (F, F), F ** -0.5, 0.375, (), jnp.float32)
    bias = normal_values(splits[5], (F,), 0.5, 3.0, (), jnp.float32)
    cotangent = normal_values(splits[6], (NODES, F), 1.0, 6.0, ((0, 8),), jnp.float32)
    return {"features": features, "tile_values": tile_values, "tile_rows": tile_rows, "tile_cols": tile_cols, "weight": weight, "bias": bias, "cotangent": cotangent}


def reference(features, tile_values, tile_rows, tile_cols, weight, bias, cotangent):
    highest = lax.Precision.HIGHEST
    col_blocks = features.reshape(COL_BLOCKS, TILE, F)
    block_ids = jnp.arange(ROW_BLOCKS, dtype=jnp.int32)

    def aggregate(part_index):
        values = tile_values[part_index].astype(jnp.float32)
        picked = col_blocks[tile_cols[part_index]]
        products = jnp.einsum("sij,sjf->sif", values, picked, precision=highest)
        select = (tile_rows[part_index][None, :] == block_ids[:, None]).astype(jnp.float32)
        return jnp.einsum("bs,sif->bif", select, products, precision=highest).reshape(ROWS, F)

    aggregated = lax.map(aggregate, jnp.arange(PARTS_SIZE, dtype=jnp.int32)).reshape(NODES, F)
    before = jnp.dot(aggregated, weight, precision=highest) + bias
    gate_value = jax.nn.sigmoid(before)
    activations = before * gate_value
    grad_pre = cotangent * gate_value * (1.0 + before * (1.0 - gate_value))
    grad_weight = jnp.dot(aggregated.T, grad_pre, precision=highest)
    grad_bias = jnp.sum(grad_pre, axis=0)
    messages = jnp.dot(grad_pre, weight.T, precision=highest).reshape(PARTS_SIZE, ROW_BLOCKS, TILE, F)
    share_values = tile_values.reshape(PARTS_SIZE, N_REP, SLOTS, TILE, TILE)
    share_rows = tile_rows.reshape(PARTS_SIZE, N_REP, SLOTS)
    share_cols = tile_cols.reshape(PARTS_SIZE, N_REP, SLOTS)
    target_ids = jnp.arange(COL_BLOCKS, dtype=jnp.int32)

    def per_part(total, part_index):
        message_blocks = messages[part_index]

        def per_share(running, share_index):
            values = share_values[part_index, share_index].astype(jnp.float32)
            picked = message_blocks[share_rows[part_index, share_index]]
            returned = jnp.einsum("sji,sjf->sif", values, picked, precision=highest)
            select = (share_cols[part_index, share_index][None, :] == target_ids[:, None]).astype(jnp.float32)
            term = jnp.einsum("ns,sif->nif", select, returned, precision=highest)
            return running + term, None

        total, unused = lax.scan(per_share, total, jnp.arange(N_REP, dtype=jnp.int32))
        return total, None

    grad_features, unused = lax.scan(per_part, jnp.zeros((COL_BLOCKS, TILE, F), jnp.float32), jnp.arange(PARTS_SIZE, dtype=jnp.int32))
    return activations, grad_features.reshape(NODES, F), grad_weight, grad_bias
```

```python
import functools

import jax
import jax.numpy as jnp
from jax import lax
from jax.experimental import pallas as pl
from jax.experimental.pallas import tpu as pltpu
from jax.sharding import PartitionSpec as P

F32 = jnp.float32
BF16 = jnp.bfloat16


def split(x):
    high = x.astype(BF16)
    return high, (x - high.astype(F32)).astype(BF16)


def mm(a, b, dims=((1,), (0,))):
    return lax.dot_general(a, b, (dims, ((), ())), preferred_element_type=F32)


def mm3(a, b, dims=((1,), (0,))):
    return mm(a[0], b[0], dims) + (mm(a[0], b[1], dims) + mm(a[1], b[0], dims))


def kernel(
    D, R, K,
    rows_ref, cols_ref, feat_ref, tiles_ref, weight_ref, bias_ref, cot_ref,
    act_ref, gfeat_ref, gweight_ref, gbias_ref,
    adj, adj_t, fbuf, part, rsbuf, agg, wterm, w1s, w1r, w2b, w3b,
    psend, precv, csend, crecv, srcp, rs2, gbuf,
    a_s, a_r, l_s, l_r, b_s, b_r, g_s, g_r,
    p_s, p_r, c_s, c_r, d_s, d_r, e_s, e_r,
    w1_s, w1_r, w2_s, w2_r, w3_s, w3_r,
):
    C = D // 2
    tile = tiles_ref.shape[2]
    slots = tiles_ref.shape[1]
    n_rows, feat = feat_ref.shape
    per = n_rows // tile
    half = feat // 2
    piece = w1s.shape[1] - 8
    d = lax.axis_index("dom")
    r = lax.axis_index("rep")
    chip, core = d // 2, d % 2
    other = 1 - core
    partner = chip * 2 + other

    def dom_at(k):
        return lax.rem(d + k, D)

    def rep_at(k):
        return lax.rem(r + k, R)

    def chip_at(k):
        return lax.rem(chip + k, C)

    def copy(src, dst, ss, rs, dom=None, rep=None):
        return pltpu.make_async_remote_copy(
            src_ref=src, dst_ref=dst, send_sem=ss, recv_sem=rs,
            device_id={"dom": d if dom is None else dom, "rep": r if rep is None else rep},
            device_id_type=pl.DeviceIdType.MESH,
        )

    sent = []

    def send(*args, **kw):
        c = copy(*args, **kw)
        c.start()
        sent.append(c)
        return c

    barrier = pltpu.get_barrier_semaphore()
    for k in range(1, D):
        pl.semaphore_signal(barrier, inc=1, device_id={"dom": dom_at(k), "rep": r}, device_id_type=pl.DeviceIdType.MESH)
    for k in range(1, R):
        pl.semaphore_signal(barrier, inc=1, device_id={"dom": d, "rep": rep_at(k)}, device_id_type=pl.DeviceIdType.MESH)
    pl.semaphore_wait(barrier, D - 1 + R - 1)

    lanes = [pl.ds(h * half, half) for h in range(2)]
    gather = {}
    relay = {}
    for h in range(2):
        own = feat_ref.at[:, lanes[h]]
        relay[h, 0] = send(own, fbuf.at[h, 0, 1], l_s.at[h, 0], l_r.at[h, 0], dom=partner)
        for k in range(1, C):
            gather[h, k] = send(own, fbuf.at[h, k, 0], a_s.at[h, k], a_r.at[h, k], dom=chip_at(k) * 2 + core)

    def place(q, carry):
        for j in range(per):
            col = q * per + j
            slot = jnp.int32(0)
            for s in range(slots):
                slot = jnp.where(cols_ref[0, s] == col, jnp.int32(s), slot)
            row = rows_ref[0, slot]
            values = tiles_ref[0, slot].astype(F32)
            turned = values.T
            for b in range(per):
                keep = jnp.where(row == b, jnp.float32(1), jnp.float32(0))
                adj[q, pl.ds(b * tile, tile), pl.ds(j * tile, tile)] = (values * keep).astype(BF16)
                adj_t[q, pl.ds(j * tile, tile), pl.ds(b * tile, tile)] = (turned * keep).astype(BF16)
        return carry

    lax.fori_loop(0, D, place, 0)
    w = split(weight_ref[...])

    def product(matrix, block):
        high, low = split(block)
        both = mm(matrix, jnp.concatenate([high, low], axis=1))
        return both[:, :half] + both[:, half:]

    reduce_rows = n_rows // R

    def rep_reduce(h, source, buf, ss, rs):
        return [
            send(source.at[h, rep_at(k)], buf.at[h, k], ss.at[h, k], rs.at[h, k], rep=rep_at(k))
            for k in range(1, R)
        ]

    def rep_gather(h, copies, source, buf, out, ss, rs):
        total = source[h, r]
        for k in range(1, R):
            copies[k - 1].wait_recv()
            total = total + buf[h, k]
        out[h, r] = total
        return [send(out.at[h, r], out.at[h, r], ss.at[h, k], rs.at[h, k], rep=rep_at(k)) for k in range(1, R)]

    before = bias_ref[...]
    reduces = []
    gathers = []
    for h in range(2):
        total = product(adj[d], feat_ref[:, h * half:(h + 1) * half])
        relay[h, 0].wait_recv()
        total = total + product(adj[partner], fbuf[h, 0, 1])
        for k in range(1, C):
            gather[h, k].wait_recv()
            relay[h, k] = send(fbuf.at[h, k, 0], fbuf.at[h, k, 1], l_s.at[h, k], l_r.at[h, k], dom=partner)
            source = lax.rem(chip + C - k, C)
            total = total + product(adj[source * 2 + core], fbuf[h, k, 0])
        for k in range(1, C):
            source = lax.rem(chip + C - k, C)
            relay[h, k].wait_recv()
            total = total + product(adj[source * 2 + other], fbuf[h, k, 1])
        part[h] = total.reshape(R, reduce_rows, half)
        reduces.append(rep_reduce(h, part, rsbuf, b_s, b_r))
        if h == 0:
            gathers.append(rep_gather(0, reduces[0], part, rsbuf, agg, g_s, g_r))
    gathers.append(rep_gather(1, reduces[1], part, rsbuf, agg, g_s, g_r))

    sums = []
    for h in range(2):
        for c in gathers[h]:
            c.wait_recv()
        a = split(agg[h].reshape(n_rows, half))
        sums.append(a)
        before = before + mm3(a, (w[0][h * half:(h + 1) * half], w[1][h * half:(h + 1) * half]))
    gate = 1.0 / (1.0 + jnp.exp(-before))
    act_ref[...] = before * gate
    grad_pre = cot_ref[...] * gate * (1.0 + before * (1.0 - gate))
    g = split(grad_pre)

    scatters = []
    for h in range(2):
        m = mm3(g, (w[0][h * half:(h + 1) * half], w[1][h * half:(h + 1) * half]), ((1,), (1,)))
        high, low = split(m)
        both = jnp.concatenate([high, low], axis=1)

        def back(q):
            x = mm(adj_t[q], both)
            return x[:, :half] + x[:, half:]

        order = list(range(1, C)) + [0]
        pairs = {}
        for k in order:
            psend[h, k] = back(chip_at(k) * 2 + other)
            pairs[k] = send(psend.at[h, k], precv.at[h, k], p_s.at[h, k], p_r.at[h, k], dom=partner)
        chips = []
        for k in order:
            x = back(chip_at(k) * 2 + core)
            pairs[k].wait_recv()
            csend[h, k] = x + precv[h, k]
            if k:
                chips.append(
                    send(csend.at[h, k], crecv.at[h, k], c_s.at[h, k], c_r.at[h, k], dom=chip_at(k) * 2 + core)
                )
        scatters.append(chips)

        if h == 0:
            for b in range(2):
                term = mm3(sums[b], g, ((0,), (0,)))
                count = half // piece
                wterm[pl.ds(b * count, count)] = term.reshape(count, piece, feat)
            bias_term = jnp.broadcast_to(jnp.sum(grad_pre, axis=0, keepdims=True), (8, feat))
            for o in range(K):
                w1s[o, pl.ds(0, piece)] = wterm[r * K + o]
                w1s[o, pl.ds(piece, 8)] = bias_term
            ones = []
            for k in range(1, D):
                owner = dom_at(k)
                if K == D:
                    ones.append(send(w1s.at[owner], w1r.at[k], w1_s.at[k], w1_r.at[k], dom=owner))
                else:
                    owner_in = jnp.minimum(owner, K - 1)
                    c = copy(w1s.at[owner_in], w1r.at[k], w1_s.at[k], w1_r.at[k], dom=owner)
                    ones.append(c)

                    @pl.when(owner < K)
                    def _(c=c):
                        c.start()
                        c.wait_send()

    twos = [
        copy(w2b.at[jnp.minimum(d, K - 1)], w2b.at[jnp.minimum(d, K - 1)], w2_s.at[k], w2_r.at[k], dom=dom_at(k))
        for k in range(1, D)
    ]

    def own_piece():
        total = w1s[jnp.minimum(d, K - 1)]
        for k in range(1, D):
            ones[k - 1].wait_recv()
            total = total + w1r[k]
        w2b[jnp.minimum(d, K - 1)] = total
        for c in twos:
            c.start()

    if K == D:
        own_piece()
        sent.extend(twos)
    else:
        @pl.when(d < K)
        def _():
            own_piece()
            for c in twos:
                c.wait_send()

    def back_sum(h):
        total = csend[h, 0]
        for k in range(1, C):
            scatters[h][k - 1].wait_recv()
            total = total + crecv[h, k]
        srcp[h] = total.reshape(R, reduce_rows, half)
        return rep_reduce(h, srcp, rs2, d_s, d_r)

    first = back_sum(0)

    for k in range(1, D):
        source = lax.rem(d + D - k, D)
        if K == D:
            copy(w2b.at[source], w2b.at[source], w2_s.at[k], w2_r.at[k], dom=dom_at(k)).wait_recv()
        else:
            @pl.when(source < K)
            def _(k=k, source=source):
                s = jnp.minimum(source, K - 1)
                copy(w2b.at[s], w2b.at[s], w2_s.at[k], w2_r.at[k], dom=dom_at(k)).wait_recv()
    w3b[r] = w2b[:, :piece].reshape(K * piece, feat)
    threes = [send(w3b.at[r], w3b.at[r], w3_s.at[k], w3_r.at[k], rep=rep_at(k)) for k in range(1, R)]
    gbias_ref[...] = w2b[0, piece:piece + 1]

    ends = [rep_gather(0, first, srcp, rs2, gbuf, e_s, e_r)]
    second = back_sum(1)
    ends.append(rep_gather(1, second, srcp, rs2, gbuf, e_s, e_r))
    for c in threes:
        c.wait_recv()
    gweight_ref[...] = w3b[...].reshape(feat, feat)
    for h in range(2):
        for c in ends[h]:
            c.wait_recv()
        gfeat_ref[:, h * half:(h + 1) * half] = gbuf[h].reshape(n_rows, half)
    for c in sent:
        c.wait_send()


def body(D, R, features, tile_values, tile_rows, tile_cols, weight, bias, cotangent):
    n_rows, feat = features.shape
    half = feat // 2
    C = D // 2
    share = feat // R
    K = min(D, share // 8)
    piece = share // K
    chunk = n_rows // R
    vmem = pl.BlockSpec(memory_space=pltpu.VMEM)
    smem = pl.BlockSpec(memory_space=pltpu.SMEM)

    def sems(*shape):
        return pltpu.SemaphoreType.DMA(shape)

    out = pl.pallas_call(
        functools.partial(kernel, D, R, K),
        out_shape=(
            jax.ShapeDtypeStruct((n_rows, feat), F32),
            jax.ShapeDtypeStruct((n_rows, feat), F32),
            jax.ShapeDtypeStruct((feat, feat), F32),
            jax.ShapeDtypeStruct((1, feat), F32),
        ),
        in_specs=[smem, smem] + [vmem] * 5,
        out_specs=(vmem,) * 4,
        scratch_shapes=[
            pltpu.VMEM((D, n_rows, n_rows), BF16),
            pltpu.VMEM((D, n_rows, n_rows), BF16),
            pltpu.VMEM((2, C, 2, n_rows, half), F32),
            pltpu.VMEM((2, R, chunk, half), F32),
            pltpu.VMEM((2, R, chunk, half), F32),
            pltpu.VMEM((2, R, chunk, half), F32),
            pltpu.VMEM((R * K, piece, feat), F32),
            pltpu.VMEM((K, piece + 8, feat), F32),
            pltpu.VMEM((D, piece + 8, feat), F32),
            pltpu.VMEM((K, piece + 8, feat), F32),
            pltpu.VMEM((R, share, feat), F32),
            pltpu.VMEM((2, C, n_rows, half), F32),
            pltpu.VMEM((2, C, n_rows, half), F32),
            pltpu.VMEM((2, C, n_rows, half), F32),
            pltpu.VMEM((2, C, n_rows, half), F32),
            pltpu.VMEM((2, R, chunk, half), F32),
            pltpu.VMEM((2, R, chunk, half), F32),
            pltpu.VMEM((2, R, chunk, half), F32),
        ]
        + [sems(2, C)] * 4
        + [sems(2, R)] * 4
        + [sems(2, C)] * 4
        + [sems(2, R)] * 4
        + [sems(D)] * 4
        + [sems(R)] * 2,
        compiler_params=pltpu.CompilerParams(
            collective_id=0, has_side_effects=True, vmem_limit_bytes=56 * 1024 * 1024
        ),
        name="layer",
    )(tile_rows, tile_cols, features, tile_values, weight, bias.reshape(1, feat), cotangent)
    activations, grad_features, grad_weight, grad_bias = out
    return activations, grad_features, grad_weight, grad_bias.reshape(feat)


def solution(mesh):
    D, R = mesh.shape["dom"], mesh.shape["rep"]
    return jax.shard_map(
        functools.partial(body, D, R),
        mesh=mesh,
        in_specs=(
            P("dom", None),
            P("dom", "rep", None, None),
            P("dom", "rep"),
            P("dom", "rep"),
            P(),
            P(),
            P("dom", None),
        ),
        out_specs=(P("dom", None), P("dom", None), P(), P()),
        check_vma=False,
    )
```

```python
import functools

import jax
import jax.numpy as jnp
from jax import lax
from jax.experimental import pallas as pl
from jax.experimental.pallas import tpu as pltpu
from jax.sharding import PartitionSpec as P

F32 = jnp.float32
BF16 = jnp.bfloat16


def split(x):
    high = x.astype(BF16)
    return high, (x - high.astype(F32)).astype(BF16)


def mm(a, b, dims=((1,), (0,))):
    return lax.dot_general(a, b, (dims, ((), ())), preferred_element_type=F32)


def mm3(a, b, dims=((1,), (0,))):
    return mm(a[0], b[0], dims) + (mm(a[0], b[1], dims) + mm(a[1], b[0], dims))


def kernel(
    D, R, K,
    rows_ref, cols_ref, feat_ref, tiles_ref, weight_ref, bias_ref, cot_ref,
    act_ref, gfeat_ref, gweight_ref, gbias_ref,
    adj, adj_t, fbuf, part, rsbuf, agg, wterm, w1s, w1r, w2b, w3b,
    psend, precv, csend, crecv, srcp, rs2, gbuf,
    a_s, a_r, l_s, l_r, b_s, b_r, g_s, g_r,
    p_s, p_r, c_s, c_r, d_s, d_r, e_s, e_r,
    w1_s, w1_r, w2_s, w2_r, w3_s, w3_r, w4_s, w4_r,
):
    C = D // 2
    tile = tiles_ref.shape[2]
    slots = tiles_ref.shape[1]
    n_rows, feat = feat_ref.shape
    per = n_rows // tile
    half = feat // 2
    piece = w1s.shape[1] - 8
    d = lax.axis_index("dom")
    r = lax.axis_index("rep")
    chip, core = d // 2, d % 2
    other = 1 - core
    partner = chip * 2 + other

    def dom_at(k):
        return lax.rem(d + k, D)

    def rep_at(k):
        return lax.rem(r + k, R)

    def chip_at(k):
        return lax.rem(chip + k, C)

    def copy(src, dst, ss, rs, dom=None, rep=None):
        return pltpu.make_async_remote_copy(
            src_ref=src, dst_ref=dst, send_sem=ss, recv_sem=rs,
            device_id={"dom": d if dom is None else dom, "rep": r if rep is None else rep},
            device_id_type=pl.DeviceIdType.MESH,
        )

    sent = []

    def send(*args, **kw):
        c = copy(*args, **kw)
        c.start()
        sent.append(c)
        return c

    barrier = pltpu.get_barrier_semaphore()
    for k in range(1, D):
        pl.semaphore_signal(barrier, inc=1, device_id={"dom": dom_at(k), "rep": r}, device_id_type=pl.DeviceIdType.MESH)
    for k in range(1, R):
        pl.semaphore_signal(barrier, inc=1, device_id={"dom": d, "rep": rep_at(k)}, device_id_type=pl.DeviceIdType.MESH)
    pl.semaphore_wait(barrier, D - 1 + R - 1)

    lanes = [pl.ds(h * half, half) for h in range(2)]
    gather = {}
    relay = {}
    for h in range(2):
        own = feat_ref.at[:, lanes[h]]
        relay[h, 0] = send(own, fbuf.at[h, 0, 1], l_s.at[h, 0], l_r.at[h, 0], dom=partner)
        for k in range(1, C):
            gather[h, k] = copy(own, fbuf.at[h, k, 0], a_s.at[h, k], a_r.at[h, k], dom=chip_at(k) * 2 + core)
    for k in range(1, C):
        gather[0, k].start()

    def place(q, carry):
        for j in range(per):
            col = q * per + j
            slot = jnp.int32(0)
            for s in range(slots):
                slot = jnp.where(cols_ref[0, s] == col, jnp.int32(s), slot)
            row = rows_ref[0, slot]
            values = tiles_ref[0, slot].astype(F32)
            turned = values.T
            for b in range(per):
                keep = jnp.where(row == b, jnp.float32(1), jnp.float32(0))
                adj[q, pl.ds(b * tile, tile), pl.ds(j * tile, tile)] = (values * keep).astype(BF16)
                adj_t[q, pl.ds(j * tile, tile), pl.ds(b * tile, tile)] = (turned * keep).astype(BF16)
        return carry

    lax.fori_loop(0, D, place, 0)
    w = split(weight_ref[...])
    for k in range(1, C):
        gather[0, k].wait_send()
        gather[1, k].start()
        sent.append(gather[1, k])

    def product(matrix, block):
        high, low = split(block)
        both = mm(matrix, jnp.concatenate([high, low], axis=1))
        return both[:, :half] + both[:, half:]

    reduce_rows = n_rows // R

    def rep_reduce(h, source, buf, ss, rs):
        return [
            send(source.at[h, rep_at(k)], buf.at[h, k], ss.at[h, k], rs.at[h, k], rep=rep_at(k))
            for k in range(1, R)
        ]

    def rep_gather(h, copies, source, buf, out, ss, rs):
        total = source[h, r]
        for k in range(1, R):
            copies[k - 1].wait_recv()
            total = total + buf[h, k]
        out[h, r] = total
        return [send(out.at[h, r], out.at[h, r], ss.at[h, k], rs.at[h, k], rep=rep_at(k)) for k in range(1, R)]

    before = bias_ref[...]
    reduces = []
    gathers = []
    for h in range(2):
        total = product(adj[d], feat_ref[:, h * half:(h + 1) * half])
        relay[h, 0].wait_recv()
        total = total + product(adj[partner], fbuf[h, 0, 1])
        for k in range(1, C):
            gather[h, k].wait_recv()
            relay[h, k] = send(fbuf.at[h, k, 0], fbuf.at[h, k, 1], l_s.at[h, k], l_r.at[h, k], dom=partner)
            source = lax.rem(chip + C - k, C)
            total = total + product(adj[source * 2 + core], fbuf[h, k, 0])
        for k in range(1, C):
            source = lax.rem(chip + C - k, C)
            relay[h, k].wait_recv()
            total = total + product(adj[source * 2 + other], fbuf[h, k, 1])
        part[h] = total.reshape(R, reduce_rows, half)
        reduces.append(rep_reduce(h, part, rsbuf, b_s, b_r))
        if h == 0:
            gathers.append(rep_gather(0, reduces[0], part, rsbuf, agg, g_s, g_r))
    gathers.append(rep_gather(1, reduces[1], part, rsbuf, agg, g_s, g_r))

    sums = []
    for h in range(2):
        for c in gathers[h]:
            c.wait_recv()
        a = split(agg[h].reshape(n_rows, half))
        sums.append(a)
        before = before + mm3(a, (w[0][h * half:(h + 1) * half], w[1][h * half:(h + 1) * half]))
    gate = 1.0 / (1.0 + jnp.exp(-before))
    act_ref[...] = before * gate
    grad_pre = cot_ref[...] * gate * (1.0 + before * (1.0 - gate))
    g = split(grad_pre)

    order = list(range(1, C)) + [0]

    def message_half(h):
        m = mm3(g, (w[0][h * half:(h + 1) * half], w[1][h * half:(h + 1) * half]), ((1,), (1,)))
        return jnp.concatenate(split(m), axis=1)

    def back(both, q):
        x = mm(adj_t[q], both)
        return x[:, :half] + x[:, half:]

    def pair_half(h, both):
        pairs = {}
        for k in order:
            psend[h, k] = back(both, chip_at(k) * 2 + other)
            pairs[k] = send(psend.at[h, k], precv.at[h, k], p_s.at[h, k], p_r.at[h, k], dom=partner)
        return pairs

    def chip_half(h, both, pairs, earlier):
        copies = []
        for k in order:
            x = back(both, chip_at(k) * 2 + core)
            pairs[k].wait_recv()
            csend[h, k] = x + precv[h, k]
            if k:
                c = copy(csend.at[h, k], crecv.at[h, k], c_s.at[h, k], c_r.at[h, k], dom=chip_at(k) * 2 + core)
                if earlier is not None:
                    earlier[k - 1].wait_send()
                c.start()
                copies.append(c)
        return copies

    scatters = []
    both = message_half(0)
    pairs = pair_half(0, both)
    scatters.append(chip_half(0, both, pairs, None))
    both = message_half(1)
    pairs = pair_half(1, both)

    for b in range(2):
        term = mm3(sums[b], g, ((0,), (0,)))
        count = half // piece
        wterm[pl.ds(b * count, count)] = term.reshape(count, piece, feat)
    bias_term = jnp.broadcast_to(jnp.sum(grad_pre, axis=0, keepdims=True), (8, feat))
    for o in range(K):
        w1s[o, pl.ds(0, piece)] = wterm[r * K + o]
        w1s[o, pl.ds(piece, 8)] = bias_term
    ones = [
        send(w1s.at[jnp.minimum(dom_at(k), K - 1)], w1r.at[k], w1_s.at[k], w1_r.at[k], dom=dom_at(k))
        for k in range(1, D)
    ]
    scatters.append(chip_half(1, both, pairs, scatters[0]))
    sent.extend(scatters[1])

    total = w1s[jnp.minimum(d, K - 1)]
    for k in range(1, D):
        ones[k - 1].wait_recv()
        total = total + w1r[k]
    gbias_ref[...] = total[piece:piece + 1]
    w2b[r] = total[:piece]
    twos = [send(w2b.at[r], w2b.at[r], w2_s.at[k], w2_r.at[k], rep=rep_at(k)) for k in range(1, R)]

    def back_sum(h):
        total = csend[h, 0]
        for k in range(1, C):
            scatters[h][k - 1].wait_recv()
            total = total + crecv[h, k]
        srcp[h] = total.reshape(R, reduce_rows, half)
        return rep_reduce(h, srcp, rs2, d_s, d_r)

    first = back_sum(0)

    for c in twos:
        c.wait_recv()

    def when_owner(place, action):
        if K == D:
            action()
        else:
            pl.when(place < K // 2)(action)

    def three(k, source):
        slot = jnp.minimum(source, K // 2 - 1) * 2 + core
        return copy(w3b.at[slot], w3b.at[slot], w3_s.at[k], w3_r.at[k], dom=chip_at(k) * 2 + core)

    def four(k, side):
        source = lax.rem(chip + C - k, C)
        slot = jnp.minimum(source, K // 2 - 1) * 2 + side
        return copy(w3b.at[slot], w3b.at[slot], w4_s.at[k], w4_r.at[k], dom=partner)

    def hand_out():
        w3b[jnp.minimum(chip, K // 2 - 1) * 2 + core] = w2b[...]
        for k in range(1, C):
            three(k, chip).start()
        four(0, core).start()

    when_owner(chip, hand_out)
    ends = [rep_gather(0, first, srcp, rs2, gbuf, e_s, e_r)]
    second = back_sum(1)
    for k in range(1, C):
        def pass_on(k=k):
            three(k, lax.rem(chip + C - k, C)).wait_recv()
            four(k, core).start()

        when_owner(lax.rem(chip + C - k, C), pass_on)
    ends.append(rep_gather(1, second, srcp, rs2, gbuf, e_s, e_r))
    for k in range(C):
        def take(k=k):
            four(k, other).wait_recv()
            four(k, core).wait_send()

        when_owner(lax.rem(chip + C - k, C), take)

    def handed():
        for k in range(1, C):
            three(k, chip).wait_send()

    when_owner(chip, handed)
    for b in range(R):
        for o in range(K):
            gweight_ref[pl.ds((b * K + o) * piece, piece)] = w3b[o, b]
    for h in range(2):
        for c in ends[h]:
            c.wait_recv()
        gfeat_ref[:, h * half:(h + 1) * half] = gbuf[h].reshape(n_rows, half)
    for c in sent:
        c.wait_send()


def body(D, R, features, tile_values, tile_rows, tile_cols, weight, bias, cotangent):
    n_rows, feat = features.shape
    half = feat // 2
    C = D // 2
    share = feat // R
    K = min(D, share // 8)
    piece = share // K
    chunk = n_rows // R
    vmem = pl.BlockSpec(memory_space=pltpu.VMEM)
    smem = pl.BlockSpec(memory_space=pltpu.SMEM)

    def sems(*shape):
        return pltpu.SemaphoreType.DMA(shape)

    out = pl.pallas_call(
        functools.partial(kernel, D, R, K),
        out_shape=(
            jax.ShapeDtypeStruct((n_rows, feat), F32),
            jax.ShapeDtypeStruct((n_rows, feat), F32),
            jax.ShapeDtypeStruct((feat, feat), F32),
            jax.ShapeDtypeStruct((1, feat), F32),
        ),
        in_specs=[smem, smem] + [vmem] * 5,
        out_specs=(vmem,) * 4,
        scratch_shapes=[
            pltpu.VMEM((D, n_rows, n_rows), BF16),
            pltpu.VMEM((D, n_rows, n_rows), BF16),
            pltpu.VMEM((2, C, 2, n_rows, half), F32),
            pltpu.VMEM((2, R, chunk, half), F32),
            pltpu.VMEM((2, R, chunk, half), F32),
            pltpu.VMEM((2, R, chunk, half), F32),
            pltpu.VMEM((R * K, piece, feat), F32),
            pltpu.VMEM((K, piece + 8, feat), F32),
            pltpu.VMEM((D, piece + 8, feat), F32),
            pltpu.VMEM((R, piece, feat), F32),
            pltpu.VMEM((K, R, piece, feat), F32),
            pltpu.VMEM((2, C, n_rows, half), F32),
            pltpu.VMEM((2, C, n_rows, half), F32),
            pltpu.VMEM((2, C, n_rows, half), F32),
            pltpu.VMEM((2, C, n_rows, half), F32),
            pltpu.VMEM((2, R, chunk, half), F32),
            pltpu.VMEM((2, R, chunk, half), F32),
            pltpu.VMEM((2, R, chunk, half), F32),
        ]
        + [sems(2, C)] * 4
        + [sems(2, R)] * 4
        + [sems(2, C)] * 4
        + [sems(2, R)] * 4
        + [sems(D)] * 2
        + [sems(R)] * 2
        + [sems(C)] * 4,
        compiler_params=pltpu.CompilerParams(
            collective_id=0, has_side_effects=True, vmem_limit_bytes=56 * 1024 * 1024
        ),
        name="layer",
    )(tile_rows, tile_cols, features, tile_values, weight, bias.reshape(1, feat), cotangent)
    activations, grad_features, grad_weight, grad_bias = out
    return activations, grad_features, grad_weight, grad_bias.reshape(feat)


def solution(mesh):
    D, R = mesh.shape["dom"], mesh.shape["rep"]
    return jax.shard_map(
        functools.partial(body, D, R),
        mesh=mesh,
        in_specs=(
            P("dom", None),
            P("dom", "rep", None, None),
            P("dom", "rep"),
            P("dom", "rep"),
            P(),
            P(),
            P("dom", None),
        ),
        out_specs=(P("dom", None), P("dom", None), P(), P()),
        check_vma=False,
    )
```

```python
import functools

import jax
import jax.numpy as jnp
from jax import lax
from jax.experimental import pallas as pl
from jax.experimental.pallas import tpu as pltpu
from jax.sharding import PartitionSpec as P

F32 = jnp.float32
BF16 = jnp.bfloat16


def split(x):
    high = x.astype(BF16)
    return high, (x - high.astype(F32)).astype(BF16)


def mm(a, b, dims=((1,), (0,))):
    return lax.dot_general(a, b, (dims, ((), ())), preferred_element_type=F32)


def mm3(a, b, dims=((1,), (0,))):
    return mm(a[0], b[0], dims) + (mm(a[0], b[1], dims) + mm(a[1], b[0], dims))


def kernel(
    D, R, K,
    rows_ref, cols_ref, feat_ref, tiles_ref, weight_ref, bias_ref, cot_ref,
    act_ref, gfeat_ref, gweight_ref, gbias_ref,
    adj, adj_t, fbuf, part, rsbuf, agg, wterm, w1s, w1r, w2b, w3b,
    psend, precv, csend, crecv, srcp, rs2, gbuf,
    a_s, a_r, l_s, l_r, b_s, b_r, g_s, g_r,
    p_s, p_r, c_s, c_r, d_s, d_r, e_s, e_r,
    w1_s, w1_r, w2_s, w2_r, w3_s, w3_r, w4_s, w4_r,
):
    C = D // 2
    tile = tiles_ref.shape[2]
    slots = tiles_ref.shape[1]
    n_rows, feat = feat_ref.shape
    per = n_rows // tile
    half = feat // 2
    piece = w1s.shape[1] - 8
    d = lax.axis_index("dom")
    r = lax.axis_index("rep")
    chip, core = d // 2, d % 2
    other = 1 - core
    partner = chip * 2 + other

    def dom_at(k):
        return lax.rem(d + k, D)

    def rep_at(k):
        return lax.rem(r + k, R)

    def chip_at(k):
        return lax.rem(chip + k, C)

    def copy(src, dst, ss, rs, dom=None, rep=None):
        return pltpu.make_async_remote_copy(
            src_ref=src, dst_ref=dst, send_sem=ss, recv_sem=rs,
            device_id={"dom": d if dom is None else dom, "rep": r if rep is None else rep},
            device_id_type=pl.DeviceIdType.MESH,
        )

    sent = []

    def send(*args, **kw):
        c = copy(*args, **kw)
        c.start()
        sent.append(c)
        return c

    barrier = pltpu.get_barrier_semaphore()
    for k in range(1, D):
        pl.semaphore_signal(barrier, inc=1, device_id={"dom": dom_at(k), "rep": r}, device_id_type=pl.DeviceIdType.MESH)
    for k in range(1, R):
        pl.semaphore_signal(barrier, inc=1, device_id={"dom": d, "rep": rep_at(k)}, device_id_type=pl.DeviceIdType.MESH)
    pl.semaphore_wait(barrier, D - 1 + R - 1)

    lanes = [pl.ds(h * half, half) for h in range(2)]
    gather = {}
    relay = {}
    for h in range(2):
        own = feat_ref.at[:, lanes[h]]
        relay[h, 0] = send(own, fbuf.at[h, 0, 1], l_s.at[h, 0], l_r.at[h, 0], dom=partner)
        for k in range(1, C):
            gather[h, k] = copy(own, fbuf.at[h, k, 0], a_s.at[h, k], a_r.at[h, k], dom=chip_at(k) * 2 + core)
    for k in range(1, C):
        gather[0, k].start()

    def place(q, carry):
        for j in range(per):
            col = q * per + j
            slot = jnp.int32(0)
            for s in range(slots):
                slot = jnp.where(cols_ref[0, s] == col, jnp.int32(s), slot)
            row = rows_ref[0, slot]
            values = tiles_ref[0, slot].astype(F32)
            turned = values.T
            for b in range(per):
                keep = jnp.where(row == b, jnp.float32(1), jnp.float32(0))
                adj[q, pl.ds(b * tile, tile), pl.ds(j * tile, tile)] = (values * keep).astype(BF16)
                adj_t[q, pl.ds(j * tile, tile), pl.ds(b * tile, tile)] = (turned * keep).astype(BF16)
        return carry

    lax.fori_loop(0, D, place, 0)
    w = split(weight_ref[...])
    for k in range(1, C):
        gather[0, k].wait_send()
        gather[1, k].start()
        sent.append(gather[1, k])

    def product(matrix, block):
        high, low = split(block)
        both = mm(matrix, jnp.concatenate([high, low], axis=1))
        return both[:, :half] + both[:, half:]

    reduce_rows = n_rows // R

    def rep_reduce(h, source, buf, ss, rs):
        return [
            send(source.at[h, rep_at(k)], buf.at[h, k], ss.at[h, k], rs.at[h, k], rep=rep_at(k))
            for k in range(1, R)
        ]

    def rep_gather(h, copies, source, buf, out, ss, rs):
        total = source[h, r]
        for k in range(1, R):
            copies[k - 1].wait_recv()
            total = total + buf[h, k]
        out[h, r] = total
        return [send(out.at[h, r], out.at[h, r], ss.at[h, k], rs.at[h, k], rep=rep_at(k)) for k in range(1, R)]

    before = bias_ref[...]
    reduces = []
    gathers = []
    for h in range(2):
        total = product(adj[d], feat_ref[:, h * half:(h + 1) * half])
        relay[h, 0].wait_recv()
        total = total + product(adj[partner], fbuf[h, 0, 1])
        for k in range(1, C):
            gather[h, k].wait_recv()
            relay[h, k] = send(fbuf.at[h, k, 0], fbuf.at[h, k, 1], l_s.at[h, k], l_r.at[h, k], dom=partner)
            source = lax.rem(chip + C - k, C)
            total = total + product(adj[source * 2 + core], fbuf[h, k, 0])
        if h:
            gathers.append(rep_gather(0, reduces[0], part, rsbuf, agg, g_s, g_r))
        for k in range(1, C):
            source = lax.rem(chip + C - k, C)
            relay[h, k].wait_recv()
            total = total + product(adj[source * 2 + other], fbuf[h, k, 1])
        part[h] = total.reshape(R, reduce_rows, half)
        reduces.append(rep_reduce(h, part, rsbuf, b_s, b_r))
    gathers.append(rep_gather(1, reduces[1], part, rsbuf, agg, g_s, g_r))

    sums = []
    for h in range(2):
        for c in gathers[h]:
            c.wait_recv()
        a = split(agg[h].reshape(n_rows, half))
        sums.append(a)
        before = before + mm3(a, (w[0][h * half:(h + 1) * half], w[1][h * half:(h + 1) * half]))
    gate = 1.0 / (1.0 + jnp.exp(-before))
    act_ref[...] = before * gate
    grad_pre = cot_ref[...] * gate * (1.0 + before * (1.0 - gate))
    g = split(grad_pre)

    order = list(range(1, C)) + [0]

    def message_half(h):
        m = mm3(g, (w[0][h * half:(h + 1) * half], w[1][h * half:(h + 1) * half]), ((1,), (1,)))
        return jnp.concatenate(split(m), axis=1)

    def back(both, q):
        x = mm(adj_t[q], both)
        return x[:, :half] + x[:, half:]

    def pair_half(h, both):
        pairs = {}
        for k in order:
            psend[h, k] = back(both, chip_at(k) * 2 + other)
            pairs[k] = send(psend.at[h, k], precv.at[h, k], p_s.at[h, k], p_r.at[h, k], dom=partner)
        return pairs

    def chip_half(h, both, pairs, earlier):
        copies = []
        for k in order:
            x = back(both, chip_at(k) * 2 + core)
            pairs[k].wait_recv()
            csend[h, k] = x + precv[h, k]
            if k:
                c = copy(csend.at[h, k], crecv.at[h, k], c_s.at[h, k], c_r.at[h, k], dom=chip_at(k) * 2 + core)
                if earlier is not None:
                    earlier[k - 1].wait_send()
                c.start()
                copies.append(c)
        return copies

    scatters = []
    both = message_half(0)
    pairs = pair_half(0, both)
    scatters.append(chip_half(0, both, pairs, None))
    both = message_half(1)
    pairs = pair_half(1, both)

    for b in range(2):
        term = mm3(sums[b], g, ((0,), (0,)))
        count = half // piece
        wterm[pl.ds(b * count, count)] = term.reshape(count, piece, feat)
    bias_term = jnp.broadcast_to(jnp.sum(grad_pre, axis=0, keepdims=True), (8, feat))
    for o in range(K):
        w1s[o, pl.ds(0, piece)] = wterm[r * K + o]
        w1s[o, pl.ds(piece, 8)] = bias_term
    ones = [
        send(w1s.at[jnp.minimum(dom_at(k), K - 1)], w1r.at[k], w1_s.at[k], w1_r.at[k], dom=dom_at(k))
        for k in range(1, D)
    ]
    scatters.append(chip_half(1, both, pairs, scatters[0]))
    sent.extend(scatters[1])

    total = w1s[jnp.minimum(d, K - 1)]
    for k in range(1, D):
        ones[k - 1].wait_recv()
        total = total + w1r[k]
    gbias_ref[...] = total[piece:piece + 1]
    w2b[r] = total[:piece]
    twos = [send(w2b.at[r], w2b.at[r], w2_s.at[k], w2_r.at[k], rep=rep_at(k)) for k in range(1, R)]

    def back_sum(h):
        total = csend[h, 0]
        for k in range(1, C):
            scatters[h][k - 1].wait_recv()
            total = total + crecv[h, k]
        srcp[h] = total.reshape(R, reduce_rows, half)
        return rep_reduce(h, srcp, rs2, d_s, d_r)

    first = back_sum(0)

    for c in twos:
        c.wait_recv()

    def when_owner(place, action):
        if K == D:
            action()
        else:
            pl.when(place < K // 2)(action)

    def three(k, source):
        slot = jnp.minimum(source, K // 2 - 1) * 2 + core
        return copy(w3b.at[slot], w3b.at[slot], w3_s.at[k], w3_r.at[k], dom=chip_at(k) * 2 + core)

    def four(k, side):
        source = lax.rem(chip + C - k, C)
        slot = jnp.minimum(source, K // 2 - 1) * 2 + side
        return copy(w3b.at[slot], w3b.at[slot], w4_s.at[k], w4_r.at[k], dom=partner)

    def hand_out():
        w3b[jnp.minimum(chip, K // 2 - 1) * 2 + core] = w2b[...]
        for k in range(1, C):
            three(k, chip).start()
        four(0, core).start()

    when_owner(chip, hand_out)
    ends = [rep_gather(0, first, srcp, rs2, gbuf, e_s, e_r)]
    second = back_sum(1)
    for k in range(1, C):
        def pass_on(k=k):
            three(k, lax.rem(chip + C - k, C)).wait_recv()
            four(k, core).start()

        when_owner(lax.rem(chip + C - k, C), pass_on)
    ends.append(rep_gather(1, second, srcp, rs2, gbuf, e_s, e_r))
    for k in range(C):
        def take(k=k):
            four(k, other).wait_recv()
            four(k, core).wait_send()

        when_owner(lax.rem(chip + C - k, C), take)

    def handed():
        for k in range(1, C):
            three(k, chip).wait_send()

    when_owner(chip, handed)
    for b in range(R):
        for o in range(K):
            gweight_ref[pl.ds((b * K + o) * piece, piece)] = w3b[o, b]
    for h in range(2):
        for c in ends[h]:
            c.wait_recv()
        gfeat_ref[:, h * half:(h + 1) * half] = gbuf[h].reshape(n_rows, half)
    for c in sent:
        c.wait_send()


def store(*refs):
    for source, target in zip(refs[:4], refs[4:]):
        target[...] = source[...]


def body(D, R, features, tile_values, tile_rows, tile_cols, weight, bias, cotangent):
    n_rows, feat = features.shape
    half = feat // 2
    C = D // 2
    share = feat // R
    K = min(D, share // 8)
    piece = share // K
    chunk = n_rows // R
    vmem = pl.BlockSpec(memory_space=pltpu.VMEM)
    smem = pl.BlockSpec(memory_space=pltpu.SMEM)

    def sems(*shape):
        return pltpu.SemaphoreType.DMA(shape)

    out = pl.pallas_call(
        functools.partial(kernel, D, R, K),
        out_shape=(
            jax.ShapeDtypeStruct((n_rows, feat), F32),
            jax.ShapeDtypeStruct((n_rows, feat), F32),
            jax.ShapeDtypeStruct((feat, feat), F32),
            jax.ShapeDtypeStruct((1, feat), F32),
        ),
        in_specs=[smem, smem] + [vmem] * 5,
        out_specs=(vmem,) * 4,
        scratch_shapes=[
            pltpu.VMEM((D, n_rows, n_rows), BF16),
            pltpu.VMEM((D, n_rows, n_rows), BF16),
            pltpu.VMEM((2, C, 2, n_rows, half), F32),
            pltpu.VMEM((2, R, chunk, half), F32),
            pltpu.VMEM((2, R, chunk, half), F32),
            pltpu.VMEM((2, R, chunk, half), F32),
            pltpu.VMEM((R * K, piece, feat), F32),
            pltpu.VMEM((K, piece + 8, feat), F32),
            pltpu.VMEM((D, piece + 8, feat), F32),
            pltpu.VMEM((R, piece, feat), F32),
            pltpu.VMEM((K, R, piece, feat), F32),
            pltpu.VMEM((2, C, n_rows, half), F32),
            pltpu.VMEM((2, C, n_rows, half), F32),
            pltpu.VMEM((2, C, n_rows, half), F32),
            pltpu.VMEM((2, C, n_rows, half), F32),
            pltpu.VMEM((2, R, chunk, half), F32),
            pltpu.VMEM((2, R, chunk, half), F32),
            pltpu.VMEM((2, R, chunk, half), F32),
        ]
        + [sems(2, C)] * 4
        + [sems(2, R)] * 4
        + [sems(2, C)] * 4
        + [sems(2, R)] * 4
        + [sems(D)] * 2
        + [sems(R)] * 2
        + [sems(C)] * 4,
        compiler_params=pltpu.CompilerParams(
            collective_id=0, has_side_effects=True, vmem_limit_bytes=56 * 1024 * 1024
        ),
        name="layer",
    )(tile_rows, tile_cols, features, tile_values, weight, bias.reshape(1, feat), cotangent)
    out = pl.pallas_call(
        store,
        out_shape=tuple(jax.ShapeDtypeStruct(x.shape, F32) for x in out),
        in_specs=[vmem] * 4,
        out_specs=(vmem,) * 4,
        name="store",
    )(*out)
    activations, grad_features, grad_weight, grad_bias = out
    return activations, grad_features, grad_weight, grad_bias.reshape(feat)


def solution(mesh):
    D, R = mesh.shape["dom"], mesh.shape["rep"]
    return jax.shard_map(
        functools.partial(body, D, R),
        mesh=mesh,
        in_specs=(
            P("dom", None),
            P("dom", "rep", None, None),
            P("dom", "rep"),
            P("dom", "rep"),
            P(),
            P(),
            P("dom", None),
        ),
        out_specs=(P("dom", None), P("dom", None), P(), P()),
        check_vma=False,
    )
```

```python
import functools

import jax
import jax.numpy as jnp
from jax import lax
from jax.experimental import pallas as pl
from jax.experimental.pallas import tpu as pltpu
from jax.sharding import PartitionSpec as P

F32 = jnp.float32
BF16 = jnp.bfloat16


def split(x):
    high = x.astype(BF16)
    return high, (x - high.astype(F32)).astype(BF16)


def mm(a, b, dims=((1,), (0,))):
    return lax.dot_general(a, b, (dims, ((), ())), preferred_element_type=F32)


def mm3(a, b, dims=((1,), (0,))):
    return mm(a[0], b[0], dims) + (mm(a[0], b[1], dims) + mm(a[1], b[0], dims))


def kernel(
    D, R, K,
    rows_ref, cols_ref, feat_ref, tiles_hbm, weight_hbm, bias_ref, cot_hbm,
    act_ref, gfeat_ref, gweight_ref, gbias_ref,
    tiles_ref, weight_ref, cot_ref, in_s, adj, adj_t, fbuf, part, rsbuf, agg, wterm, w1s, w1r, w2b, w3b,
    psend, precv, csend, crecv, srcp, rs2, gbuf,
    a_s, a_r, l_s, l_r, b_s, b_r, g_s, g_r,
    p_s, p_r, c_s, c_r, d_s, d_r, e_s, e_r,
    w1_s, w1_r, w2_s, w2_r, w3_s, w3_r, w4_s, w4_r,
):
    C = D // 2
    tile = tiles_ref.shape[2]
    slots = tiles_ref.shape[1]
    n_rows, feat = feat_ref.shape
    per = n_rows // tile
    half = feat // 2
    piece = w1s.shape[1] - 8
    d = lax.axis_index("dom")
    r = lax.axis_index("rep")
    chip, core = d // 2, d % 2
    other = 1 - core
    partner = chip * 2 + other

    def dom_at(k):
        return lax.rem(d + k, D)

    def rep_at(k):
        return lax.rem(r + k, R)

    def chip_at(k):
        return lax.rem(chip + k, C)

    def copy(src, dst, ss, rs, dom=None, rep=None):
        return pltpu.make_async_remote_copy(
            src_ref=src, dst_ref=dst, send_sem=ss, recv_sem=rs,
            device_id={"dom": d if dom is None else dom, "rep": r if rep is None else rep},
            device_id_type=pl.DeviceIdType.MESH,
        )

    sent = []

    def send(*args, **kw):
        c = copy(*args, **kw)
        c.start()
        sent.append(c)
        return c

    loads = [
        pltpu.make_async_copy(a, b, in_s.at[i])
        for i, (a, b) in enumerate(((tiles_hbm, tiles_ref), (weight_hbm, weight_ref), (cot_hbm, cot_ref)))
    ]
    barrier = pltpu.get_barrier_semaphore()
    for k in range(1, D):
        pl.semaphore_signal(barrier, inc=1, device_id={"dom": dom_at(k), "rep": r}, device_id_type=pl.DeviceIdType.MESH)
    for k in range(1, R):
        pl.semaphore_signal(barrier, inc=1, device_id={"dom": d, "rep": rep_at(k)}, device_id_type=pl.DeviceIdType.MESH)
    for c in loads:
        c.start()
    pl.semaphore_wait(barrier, D - 1 + R - 1)

    lanes = [pl.ds(h * half, half) for h in range(2)]
    gather = {}
    relay = {}
    for h in range(2):
        own = feat_ref.at[:, lanes[h]]
        relay[h, 0] = send(own, fbuf.at[h, 0, 1], l_s.at[h, 0], l_r.at[h, 0], dom=partner)
        for k in range(1, C):
            gather[h, k] = copy(own, fbuf.at[h, k, 0], a_s.at[h, k], a_r.at[h, k], dom=chip_at(k) * 2 + core)
    for k in range(1, C):
        gather[0, k].start()

    def place(q, carry):
        for j in range(per):
            col = q * per + j
            slot = jnp.int32(0)
            for s in range(slots):
                slot = jnp.where(cols_ref[0, s] == col, jnp.int32(s), slot)
            row = rows_ref[0, slot]
            values = tiles_ref[0, slot].astype(F32)
            turned = values.T
            for b in range(per):
                keep = jnp.where(row == b, jnp.float32(1), jnp.float32(0))
                adj[q, pl.ds(b * tile, tile), pl.ds(j * tile, tile)] = (values * keep).astype(BF16)
                adj_t[q, pl.ds(j * tile, tile), pl.ds(b * tile, tile)] = (turned * keep).astype(BF16)
        return carry

    for c in loads:
        c.wait()
    lax.fori_loop(0, D, place, 0)
    w = split(weight_ref[...])
    for k in range(1, C):
        gather[0, k].wait_send()
        gather[1, k].start()
        sent.append(gather[1, k])

    def product(matrix, block):
        high, low = split(block)
        both = mm(matrix, jnp.concatenate([high, low], axis=1))
        return both[:, :half] + both[:, half:]

    reduce_rows = n_rows // R

    def rep_reduce(h, source, buf, ss, rs):
        return [
            send(source.at[h, rep_at(k)], buf.at[h, k], ss.at[h, k], rs.at[h, k], rep=rep_at(k))
            for k in range(1, R)
        ]

    def rep_gather(h, copies, source, buf, out, ss, rs):
        total = source[h, r]
        for k in range(1, R):
            copies[k - 1].wait_recv()
            total = total + buf[h, k]
        out[h, r] = total
        return [send(out.at[h, r], out.at[h, r], ss.at[h, k], rs.at[h, k], rep=rep_at(k)) for k in range(1, R)]

    before = bias_ref[...]
    reduces = []
    gathers = []
    for h in range(2):
        total = product(adj[d], feat_ref[:, h * half:(h + 1) * half])
        relay[h, 0].wait_recv()
        total = total + product(adj[partner], fbuf[h, 0, 1])
        for k in range(1, C):
            gather[h, k].wait_recv()
            relay[h, k] = send(fbuf.at[h, k, 0], fbuf.at[h, k, 1], l_s.at[h, k], l_r.at[h, k], dom=partner)
            source = lax.rem(chip + C - k, C)
            total = total + product(adj[source * 2 + core], fbuf[h, k, 0])
        if h:
            gathers.append(rep_gather(0, reduces[0], part, rsbuf, agg, g_s, g_r))
        for k in range(1, C):
            source = lax.rem(chip + C - k, C)
            relay[h, k].wait_recv()
            total = total + product(adj[source * 2 + other], fbuf[h, k, 1])
        part[h] = total.reshape(R, reduce_rows, half)
        reduces.append(rep_reduce(h, part, rsbuf, b_s, b_r))
    gathers.append(rep_gather(1, reduces[1], part, rsbuf, agg, g_s, g_r))

    sums = []
    for h in range(2):
        for c in gathers[h]:
            c.wait_recv()
        a = split(agg[h].reshape(n_rows, half))
        sums.append(a)
        before = before + mm3(a, (w[0][h * half:(h + 1) * half], w[1][h * half:(h + 1) * half]))
    gate = 1.0 / (1.0 + jnp.exp(-before))
    act_ref[...] = before * gate
    grad_pre = cot_ref[...] * gate * (1.0 + before * (1.0 - gate))
    g = split(grad_pre)

    order = list(range(1, C)) + [0]

    def message_half(h):
        m = mm3(g, (w[0][h * half:(h + 1) * half], w[1][h * half:(h + 1) * half]), ((1,), (1,)))
        return jnp.concatenate(split(m), axis=1)

    def back(both, q):
        x = mm(adj_t[q], both)
        return x[:, :half] + x[:, half:]

    def pair_half(h, both):
        pairs = {}
        for k in order:
            psend[h, k] = back(both, chip_at(k) * 2 + other)
            pairs[k] = send(psend.at[h, k], precv.at[h, k], p_s.at[h, k], p_r.at[h, k], dom=partner)
        return pairs

    def chip_half(h, both, pairs, earlier):
        copies = []
        for k in order:
            x = back(both, chip_at(k) * 2 + core)
            pairs[k].wait_recv()
            csend[h, k] = x + precv[h, k]
            if k:
                c = copy(csend.at[h, k], crecv.at[h, k], c_s.at[h, k], c_r.at[h, k], dom=chip_at(k) * 2 + core)
                if earlier is not None:
                    earlier[k - 1].wait_send()
                c.start()
                copies.append(c)
        return copies

    scatters = []
    both = message_half(0)
    pairs = pair_half(0, both)
    scatters.append(chip_half(0, both, pairs, None))
    both = message_half(1)
    pairs = pair_half(1, both)

    for b in range(2):
        term = mm3(sums[b], g, ((0,), (0,)))
        count = half // piece
        wterm[pl.ds(b * count, count)] = term.reshape(count, piece, feat)
    bias_term = jnp.broadcast_to(jnp.sum(grad_pre, axis=0, keepdims=True), (8, feat))
    for o in range(K):
        w1s[o, pl.ds(0, piece)] = wterm[r * K + o]
        w1s[o, pl.ds(piece, 8)] = bias_term
    ones = [
        send(w1s.at[jnp.minimum(dom_at(k), K - 1)], w1r.at[k], w1_s.at[k], w1_r.at[k], dom=dom_at(k))
        for k in range(1, D)
    ]
    scatters.append(chip_half(1, both, pairs, scatters[0]))
    sent.extend(scatters[1])

    def back_sum(h):
        total = csend[h, 0]
        for k in range(1, C):
            scatters[h][k - 1].wait_recv()
            total = total + crecv[h, k]
        srcp[h] = total.reshape(R, reduce_rows, half)
        return rep_reduce(h, srcp, rs2, d_s, d_r)

    first = back_sum(0)

    total = w1s[jnp.minimum(d, K - 1)]
    for k in range(1, D):
        ones[k - 1].wait_recv()
        total = total + w1r[k]
    gbias_ref[...] = total[piece:piece + 1]
    w2b[r] = total[:piece]
    twos = [send(w2b.at[r], w2b.at[r], w2_s.at[k], w2_r.at[k], rep=rep_at(k)) for k in range(1, R)]

    for c in twos:
        c.wait_recv()

    def when_owner(place, action):
        if K == D:
            action()
        else:
            pl.when(place < K // 2)(action)

    def three(k, source):
        slot = jnp.minimum(source, K // 2 - 1) * 2 + core
        return copy(w3b.at[slot], w3b.at[slot], w3_s.at[k], w3_r.at[k], dom=chip_at(k) * 2 + core)

    def four(k, side):
        source = lax.rem(chip + C - k, C)
        slot = jnp.minimum(source, K // 2 - 1) * 2 + side
        return copy(w3b.at[slot], w3b.at[slot], w4_s.at[k], w4_r.at[k], dom=partner)

    def hand_out():
        w3b[jnp.minimum(chip, K // 2 - 1) * 2 + core] = w2b[...]
        for k in range(1, C):
            three(k, chip).start()
        four(0, core).start()

    when_owner(chip, hand_out)
    ends = [rep_gather(0, first, srcp, rs2, gbuf, e_s, e_r)]
    second = back_sum(1)
    for k in range(1, C):
        def pass_on(k=k):
            three(k, lax.rem(chip + C - k, C)).wait_recv()
            four(k, core).start()

        when_owner(lax.rem(chip + C - k, C), pass_on)
    ends.append(rep_gather(1, second, srcp, rs2, gbuf, e_s, e_r))
    for k in range(C):
        def take(k=k):
            four(k, other).wait_recv()
            four(k, core).wait_send()

        when_owner(lax.rem(chip + C - k, C), take)

    def handed():
        for k in range(1, C):
            three(k, chip).wait_send()

    when_owner(chip, handed)
    for b in range(R):
        for o in range(K):
            gweight_ref[pl.ds((b * K + o) * piece, piece)] = w3b[o, b]
    for h in range(2):
        for c in ends[h]:
            c.wait_recv()
        gfeat_ref[:, h * half:(h + 1) * half] = gbuf[h].reshape(n_rows, half)
    for c in sent:
        c.wait_send()


def store(*refs):
    for source, target in zip(refs[:4], refs[4:]):
        target[...] = source[...]


def body(D, R, features, tile_values, tile_rows, tile_cols, weight, bias, cotangent):
    n_rows, feat = features.shape
    half = feat // 2
    C = D // 2
    share = feat // R
    K = min(D, share // 8)
    piece = share // K
    chunk = n_rows // R
    vmem = pl.BlockSpec(memory_space=pltpu.VMEM)
    anywhere = pl.BlockSpec(memory_space=pl.ANY)
    smem = pl.BlockSpec(memory_space=pltpu.SMEM)

    def sems(*shape):
        return pltpu.SemaphoreType.DMA(shape)

    out = pl.pallas_call(
        functools.partial(kernel, D, R, K),
        out_shape=(
            jax.ShapeDtypeStruct((n_rows, feat), F32),
            jax.ShapeDtypeStruct((n_rows, feat), F32),
            jax.ShapeDtypeStruct((feat, feat), F32),
            jax.ShapeDtypeStruct((1, feat), F32),
        ),
        in_specs=[smem, smem, vmem, anywhere, anywhere, vmem, anywhere],
        out_specs=(vmem,) * 4,
        scratch_shapes=[
            pltpu.VMEM(tile_values.shape, BF16),
            pltpu.VMEM(weight.shape, F32),
            pltpu.VMEM(cotangent.shape, F32),
            sems(3),
            pltpu.VMEM((D, n_rows, n_rows), BF16),
            pltpu.VMEM((D, n_rows, n_rows), BF16),
            pltpu.VMEM((2, C, 2, n_rows, half), F32),
            pltpu.VMEM((2, R, chunk, half), F32),
            pltpu.VMEM((2, R, chunk, half), F32),
            pltpu.VMEM((2, R, chunk, half), F32),
            pltpu.VMEM((R * K, piece, feat), F32),
            pltpu.VMEM((K, piece + 8, feat), F32),
            pltpu.VMEM((D, piece + 8, feat), F32),
            pltpu.VMEM((R, piece, feat), F32),
            pltpu.VMEM((K, R, piece, feat), F32),
            pltpu.VMEM((2, C, n_rows, half), F32),
            pltpu.VMEM((2, C, n_rows, half), F32),
            pltpu.VMEM((2, C, n_rows, half), F32),
            pltpu.VMEM((2, C, n_rows, half), F32),
            pltpu.VMEM((2, R, chunk, half), F32),
            pltpu.VMEM((2, R, chunk, half), F32),
            pltpu.VMEM((2, R, chunk, half), F32),
        ]
        + [sems(2, C)] * 4
        + [sems(2, R)] * 4
        + [sems(2, C)] * 4
        + [sems(2, R)] * 4
        + [sems(D)] * 2
        + [sems(R)] * 2
        + [sems(C)] * 4,
        compiler_params=pltpu.CompilerParams(
            collective_id=0, has_side_effects=True, vmem_limit_bytes=56 * 1024 * 1024
        ),
        name="layer",
    )(tile_rows, tile_cols, features, tile_values, weight, bias.reshape(1, feat), cotangent)
    out = pl.pallas_call(
        store,
        out_shape=tuple(jax.ShapeDtypeStruct(x.shape, F32) for x in out),
        in_specs=[vmem] * 4,
        out_specs=(vmem,) * 4,
        name="store",
    )(*out)
    activations, grad_features, grad_weight, grad_bias = out
    return activations, grad_features, grad_weight, grad_bias.reshape(feat)


def solution(mesh):
    D, R = mesh.shape["dom"], mesh.shape["rep"]
    return jax.shard_map(
        functools.partial(body, D, R),
        mesh=mesh,
        in_specs=(
            P("dom", None),
            P("dom", "rep", None, None),
            P("dom", "rep"),
            P("dom", "rep"),
            P(),
            P(),
            P("dom", None),
        ),
        out_specs=(P("dom", None), P("dom", None), P(), P()),
        check_vma=False,
    )
```
